512 devices in a mesh: section: 8 (over z_lo, x), seq: 64 (over y, z_hi, core).
Axes of the slice: x: 4, y: 8, z: 8 (z_hi: 4, z_lo: 2; z = z_hi * 2 + z_lo), core: 2. Of those that a mesh axis runs over, the one named last changes fastest.
Arguments:
- fresh_qkv: bfloat16 [8, 1024, 3, 3072], P('section', 'seq'), may hold values from -6 to 6
- stale_cache: bfloat16 [8, 64, 4, 128, 768], P('section', 'seq'), may hold values from -2.5 to 2.5
- norm_gains: float32 [8, 2, 128], P('section'), may hold values from 1 to 2.5
- hidden: bfloat16 [8, 1024, 3072], P('section', 'seq'), may hold values from -6 to 6
- gate_table: bfloat16 [8, 50, 3072], P('section'), may hold values from -4 to 4
- patch_index: int32 [8], P('section'), may hold values from 0 to 3
- step_index: int32 [8], P('section'), may hold values from 0 to 49
Outputs:
- passed: bfloat16 [8, 1024, 3072], P('section', 'seq')
The draws below stay inside these ranges and needn't reach their ends.
All inputs are finite; a program needn't handle non-finite values.
Results may differ from the reference program's by a relative error of at most 0.0095.
Values may be sent and summed in bfloat16 or wider, within the bound.
A program may use at most 64 MiB of HBM per device.

```python
import math
import jax
import jax.numpy as jnp
from jax import lax

HEADS = 24
HEAD_DIM = 128
HEAD_GROUPS = 8
PATCHES = 4
STEPS = 50
WIDTH = 3072
GROUP_HEADS = 3
GROUP_WIDTH = 384
ROWS = 128
PATCH = 1024
N_SECTION = 8
N_SEQ = 64


def with_ends(drawn, stream_key, low, high):
    extent = drawn.shape
    spot = [jax.random.randint(jax.random.fold_in(stream_key, axis), (), 0, extent[axis]) for axis in range(len(extent))]
    drawn = drawn.at[tuple(spot)].set(low)
    longest = extent.index(max(extent))
    spot[longest] = (spot[longest] + 1) % extent[longest]
    return drawn.at[tuple(spot)].set(high)


def steps_of(key, extent, cuts, smallest, largest):
    factor_of = 1.0
    for position, blocks in cuts:
        heights = jax.random.uniform(jax.random.fold_in(jax.random.fold_in(key, 6), position), (blocks,), jnp.float32, smallest / len(cuts), largest / len(cuts))
        factor_of = factor_of * jnp.repeat(jnp.exp(heights), extent[position] // blocks).reshape((-1,) + (1,) * (len(extent) - 1 - position))
    return factor_of


def gaussian(rng, extent, deviation, most, cuts=(), dtype=jnp.bfloat16):
    factor_of = steps_of(rng, extent, cuts, -0.22, 0.18) if cuts else 1.0
    array = jax.random.normal(rng, extent, jnp.float32) * deviation * factor_of
    return jnp.minimum(jnp.maximum(array, -most), most).astype(dtype)


def setup_inputs(seed: int = 0) -> dict:
    key_list = jax.random.split(jax.random.key(seed), 8)
    fresh_qkv = gaussian(key_list[0], (N_SECTION, PATCH, 3, WIDTH), 1.0, 6.0, ((0, 8), (1, 64)))
    stale_cache = jnp.clip(jax.random.uniform(key_list[1], (N_SECTION, N_SEQ, PATCHES, ROWS, 2 * GROUP_WIDTH), jnp.float32, -2.5, 2.5) * steps_of(key_list[1], (N_SECTION, N_SEQ, PATCHES, ROWS, 2 * GROUP_WIDTH), ((0, 8), (1, 64)), -0.4, 0.0), -2.5, 2.5).astype(jnp.bfloat16)
    norm_gains = jnp.clip(jnp.exp(math.log(2.5) - 0.916290732 * jax.random.uniform(key_list[2], (N_SECTION, 2, HEAD_DIM), jnp.float32) ** steps_of(key_list[2], (N_SECTION, 2, HEAD_DIM), ((0, 8),), -0.2, 0.2)), 1.0, 2.5)
    hidden = gaussian(key_list[3], (N_SECTION, PATCH, WIDTH), 1.0, 6.0, ((0, 8), (1, 64)))
    gate_table = gaussian(key_list[4], (N_SECTION, STEPS, WIDTH), 1.0, 4.0, ((0, 8),))
    patch_index = with_ends(jax.random.randint(key_list[5], (N_SECTION,), 0, PATCHES), jax.random.fold_in(key_list[5], 1), 0, PATCHES - 1).astype(jnp.int32)
    step_index = with_ends(jax.random.randint(key_list[6], (N_SECTION,), 0, STEPS), jax.random.fold_in(key_list[6], 1), 0, STEPS - 1).astype(jnp.int32)
    return {"fresh_qkv": fresh_qkv, "stale_cache": stale_cache, "norm_gains": norm_gains, "hidden": hidden, "gate_table": gate_table, "patch_index": patch_index, "step_index": step_index}


def normed(values, norm_gain):
    values = values.astype(jnp.float32)
    factor = lax.rsqrt(lax.optimization_barrier(jnp.mean(values * values, axis=-1, keepdims=True)) + 1e-06)
    return (values * factor * norm_gain).astype(jnp.bfloat16)

def head_output(pieces, keep_mask):
    queries, stale_keys, stale_values, fresh_keys, fresh_values = pieces
    factor = HEAD_DIM ** (-0.5)
    stale_weights = jnp.exp(jnp.dot(queries, stale_keys.T, preferred_element_type=jnp.float32) * factor) * keep_mask
    fresh_weights = jnp.exp(jnp.dot(queries, fresh_keys.T, preferred_element_type=jnp.float32) * factor)
    totals = lax.optimization_barrier(jnp.sum(stale_weights, axis=1)) + lax.optimization_barrier(jnp.sum(fresh_weights, axis=1))
    summed = jnp.dot(stale_weights.astype(jnp.bfloat16), stale_values, preferred_element_type=jnp.float32)
    summed = summed + jnp.dot(fresh_weights.astype(jnp.bfloat16), fresh_values, preferred_element_type=jnp.float32)
    return (summed / totals[:, None]).astype(jnp.bfloat16)

def section_output(section_id, fresh_qkv, stale_cache, norm_gains, hidden, gate_table, patch_index, step_index):
    token_groups = N_SEQ // HEAD_GROUPS
    triple = fresh_qkv[section_id].reshape(PATCH, 3, HEADS, HEAD_DIM)
    queries = normed(triple[:, 0], norm_gains[section_id, 0])
    key_normed = normed(triple[:, 1], norm_gains[section_id, 1])
    cache = stale_cache[section_id].reshape(token_groups, HEAD_GROUPS, PATCHES, ROWS, 2, GROUP_HEADS, HEAD_DIM)
    cache = cache.transpose(4, 1, 5, 2, 0, 3, 6).reshape(2, HEADS, PATCHES * token_groups * ROWS, HEAD_DIM)
    keep_mask = jnp.repeat((jnp.arange(PATCHES) != patch_index[section_id]).astype(jnp.float32), token_groups * ROWS)
    pieces = (queries.transpose(1, 0, 2), cache[0], cache[1], key_normed.transpose(1, 0, 2), triple[:, 2].transpose(1, 0, 2))
    outputs = lax.map(lambda piece: head_output(piece, keep_mask), pieces)
    attention = outputs.transpose(1, 0, 2).reshape(PATCH, WIDTH).astype(jnp.float32)
    gate_row = gate_table[section_id, step_index[section_id]].astype(jnp.float32)
    return (hidden[section_id].astype(jnp.float32) + gate_row * attention).astype(jnp.bfloat16)

def reference(fresh_qkv, stale_cache, norm_gains, hidden, gate_table, patch_index, step_index):
    mixed = [section_output(section_id, fresh_qkv, stale_cache, norm_gains, hidden, gate_table, patch_index, step_index) for section_id in range(N_SECTION)]
    return jnp.stack([mixed[(section_id - 1) % N_SECTION] for section_id in range(N_SECTION)])
```

```python
import functools

import jax
import jax.numpy as jnp
from jax import lax
from jax.experimental import pallas as pl
from jax.experimental.pallas import tpu as pltpu
from jax.sharding import PartitionSpec as P

HEADS = 24
HEAD_DIM = 128
HEAD_GROUPS = 8
MESH = pl.DeviceIdType.MESH
F32 = jnp.float32
BF16 = jnp.bfloat16


def kernel(
    sections,
    seq_count,
    fresh,
    stale,
    gains,
    hidden,
    gate,
    patch,
    step,
    out,
    raw,
    old,
    gate_all,
    gate_row,
    q_out,
    k_out,
    q_all,
    keys,
    values_t,
    v_in,
    h_in,
    part,
    back,
    send,
    mixed,
    local_sem,
    own_sem,
    first_send,
    first_recv,
    turn_send,
    turn_recv,
    back_send,
    back_recv,
    out_send,
    out_recv,
):
    groups = HEAD_GROUPS
    ring = seq_count // groups
    reach = ring // 2
    heads = q_out.shape[1]
    toks = q_out.shape[2]
    dim = HEAD_DIM
    width = heads * dim
    block = groups * toks
    stale_rows = old.shape[1]
    kept = old.shape[0] - 1
    stale_keys = kept * stale_rows

    sec = lax.axis_index("section")
    me = lax.axis_index("seq")
    y = me // groups
    a = me % groups
    up = lax.rem(y + 1, ring) * groups + a
    down = lax.rem(y + ring - 1, ring) * groups + a
    next_sec = lax.rem(sec + 1, sections)
    prev_sec = lax.rem(sec + sections - 1, sections)

    def peer(d):
        return y * groups + lax.rem(a + d, groups)

    def ring_step(d):
        return lax.rem(y + ring + 1 - 2 * d, ring) * groups + a

    raw_copy = pltpu.make_async_copy(fresh.at[0, pl.ds(0, 2)], raw, local_sem.at[0])
    raw_copy.start()

    barrier = pltpu.get_barrier_semaphore()
    for d in range(1, groups):
        pl.semaphore_signal(barrier, inc=1, device_id=(sec, peer(d)), device_id_type=MESH)
    for other in (up, down):
        pl.semaphore_signal(barrier, inc=1, device_id=(sec, other), device_id_type=MESH)
    for d in range(groups):
        pl.semaphore_signal(barrier, inc=1, device_id=(prev_sec, peer(d)), device_id_type=MESH)

    old_copy = pltpu.make_async_copy(stale.at[0, 0], old, local_sem.at[1])
    old_copy.start()
    gate_copy = pltpu.make_async_copy(gate.at[0], gate_all, local_sem.at[2])
    gate_copy.start()
    mine = pl.ds(pl.multiple_of(a * toks, toks), toks)
    my_keys = pl.ds(pl.multiple_of(stale_keys + a * toks, toks), toks)
    my_cols = pl.ds(pl.multiple_of(a * width, dim), width)
    own_v = pltpu.make_async_copy(fresh.at[0, 2, :, my_cols], v_in.at[mine], own_sem.at[0])
    own_v.start()
    own_h = pltpu.make_async_copy(hidden.at[0, :, my_cols], h_in.at[mine], own_sem.at[1])
    own_h.start()

    raw_copy.wait()

    def norm(which, stage):
        gain = gains[0, which : which + 1, :]
        for g in range(groups):
            for i in range(heads):
                col = (g * heads + i) * dim
                x = raw[which, :, col : col + dim].astype(F32)
                factor = lax.rsqrt(jnp.mean(x * x, axis=-1, keepdims=True) + 1e-06)
                stage[g, i] = (x * factor * gain).astype(BF16)

    norm(0, q_out)

    pl.semaphore_wait(barrier, 2 * groups + 1)

    def first_copy(kind, d):
        to = lax.rem(a + d, groups)
        cols = pl.ds(pl.multiple_of(to * width, dim), width)
        src, dst = (
            (lambda: q_out.at[to], lambda: q_all.at[0, :, 0, mine, :]),
            (lambda: k_out.at[to], lambda: keys.at[:, my_keys, :]),
            (lambda: fresh.at[0, 2, :, cols], lambda: v_in.at[mine]),
            (lambda: hidden.at[0, :, cols], lambda: h_in.at[mine]),
        )[kind]
        return pltpu.make_async_remote_copy(
            src_ref=src(),
            dst_ref=dst(),
            send_sem=first_send.at[kind, d],
            recv_sem=first_recv.at[kind, d],
            device_id=(sec, peer(d)),
            device_id_type=MESH,
        )

    def first_arrived(kind, d):
        source = lax.rem(a + groups - d, groups)
        rows = pl.ds(pl.multiple_of(source * toks, toks), toks)
        key_rows = pl.ds(pl.multiple_of(stale_keys + source * toks, toks), toks)
        dst = (
            lambda: q_all.at[0, :, 0, rows, :],
            lambda: keys.at[:, key_rows, :],
            lambda: v_in.at[rows],
            lambda: h_in.at[rows],
        )[kind]()
        pltpu.make_async_remote_copy(
            src_ref=dst,
            dst_ref=dst,
            send_sem=first_send.at[kind, d],
            recv_sem=first_recv.at[kind, d],
            device_id=(sec, peer(d)),
            device_id_type=MESH,
        ).wait_recv()

    for d in range(1, groups):
        first_copy(0, d).start()
    q_all[0, :, 0, mine, :] = q_out[a]
    norm(1, k_out)
    for d in range(1, groups):
        first_copy(1, d).start()
    keys[:, my_keys, :] = k_out[a]
    for kind in (2, 3):
        for d in range(1, groups):
            first_copy(kind, d).start()

    def turn(r, i, d):
        far = r + 1 == reach
        return pltpu.make_async_remote_copy(
            src_ref=q_all.at[r, i, 0 if r == 0 else d],
            dst_ref=q_all.at[0, i, 1] if far else q_all.at[r + 1, i, d],
            send_sem=turn_send.at[r, i, d],
            recv_sem=turn_recv.at[r + 1, i, 0 if far else d],
            device_id=(sec, ring_step(d)),
            device_id_type=MESH,
        )

    def turn_arrived(r, i, d):
        far = r == reach
        dst = q_all.at[0, i, 1] if far else q_all.at[r, i, d]
        pltpu.make_async_remote_copy(
            src_ref=dst,
            dst_ref=dst,
            send_sem=turn_send.at[0, i, 0],
            recv_sem=turn_recv.at[r, i, 0 if far else d],
            device_id=(sec, up),
            device_id_type=MESH,
        ).wait_recv()

    def far_way(i):
        return i % 2

    for d in range(1, groups):
        first_arrived(0, d)
    for i in range(heads):
        for d in range(2):
            turn(0, i, d).start()

    old_copy.wait()
    skip = patch[0]

    for n in range(kept):
        m = n + (n >= skip).astype(jnp.int32)
        rows = slice(n * stale_rows, (n + 1) * stale_rows)
        for i in range(heads):
            keys[i, rows, :] = old[m, :, i * dim : (i + 1) * dim]
            values_t[i, 0:dim, rows] = old[m, :, width + i * dim : width + (i + 1) * dim].T
    for i in range(heads):
        values_t[i, dim:, :] = jnp.ones_like(values_t[i, dim:, :])

    gate_copy.wait()
    picked = lax.broadcasted_iota(jnp.int32, (gate_all.shape[0], dim), 0) == step[0]
    for i in range(heads):
        cols = pl.ds(pl.multiple_of(a * width + i * dim, dim), dim)
        gate_row[i] = jnp.sum(
            jnp.where(picked, gate_all[:, cols].astype(F32), 0.0), axis=0, keepdims=True
        )

    def attend(r, i):
        q = q_all[r, i].reshape(2 * block, dim)
        scores = lax.dot_general(
            keys[i], q, (((1,), (1,)), ((), ())), preferred_element_type=F32
        )
        weights = jnp.exp(scores * (dim ** (-0.5))).astype(BF16)
        part[r, i] = jnp.dot(values_t[i], weights, preferred_element_type=F32)

    def partial_sum(r, i, d):
        return part[r, i, :, d * block : (d + 1) * block]

    def back_copy(r, i, d):
        far = r == reach
        if far:
            d = far_way(i)
        return pltpu.make_async_remote_copy(
            src_ref=send.at[0, i, 1] if far else send.at[r, i, d],
            dst_ref=back.at[r - 1, i, d],
            send_sem=back_send.at[r, i, 0 if far else d],
            recv_sem=back_recv.at[r - 1, i, d],
            device_id=(sec, ring_step(1 - d)),
            device_id_type=MESH,
        )

    def back_arrived(r, i, d):
        pltpu.make_async_remote_copy(
            src_ref=back.at[r, i, d],
            dst_ref=back.at[r, i, d],
            send_sem=back_send.at[0, i, 0],
            recv_sem=back_recv.at[r, i, d],
            device_id=(sec, up),
            device_id_type=MESH,
        ).wait_recv()

    for r in range(1, reach):

        def forward(i, carry, r=r):
            for d in range(2):
                turn_arrived(r, i, d)
                if r + 1 < reach:
                    turn(r, i, d).start()
            if r + 1 == reach:
                turn(r, i, far_way(i)).start()
            return carry

        lax.fori_loop(0, heads, forward, 0)
        if r == 1:
            own_v.wait()
            own_h.wait()
            for kind in (1, 2):
                for d in range(1, groups):
                    first_arrived(kind, d)
            for i in range(heads):
                values_t[i, 0:dim, stale_keys:] = v_in[:, i * dim : (i + 1) * dim].T

        def work(i, carry, r=r):
            attend(r, i)
            if r + 1 == reach:
                for d in range(2):

                    @pl.when(far_way(i) != d)
                    def _(d=d):
                        send[r, i, d] = partial_sum(r, i, d).astype(BF16)
                        back_copy(r, i, d).start()

            return carry

        lax.fori_loop(0, heads, work, 0)

    def far_work(i, carry):
        turn_arrived(reach, i, 0)
        attend(0, i)
        send[0, i, 1] = partial_sum(0, i, 1).astype(BF16)
        back_copy(reach, i, 0).start()
        return carry

    lax.fori_loop(0, heads, far_work, 0)

    for r in range(reach - 1, 0, -1):

        def add_on(i, carry, r=r):
            for d in range(2):

                def go(d=d):
                    back_arrived(r, i, d)
                    send[r, i, d] = (
                        partial_sum(r, i, d) + back[r, i, d].astype(F32)
                    ).astype(BF16)
                    back_copy(r, i, d).start()

                if r + 1 == reach:
                    pl.when(far_way(i) == d)(go)
                else:
                    go()
            return carry

        lax.fori_loop(0, heads, add_on, 0)

    for d in range(1, groups):
        first_arrived(3, d)

    def out_copy(i, d):
        to = lax.rem(a + d, groups)
        rows = pl.ds(pl.multiple_of(to * toks, toks), toks)
        cols = pl.ds(pl.multiple_of(a * width + i * dim, dim), dim)
        return pltpu.make_async_remote_copy(
            src_ref=mixed.at[i, rows, :],
            dst_ref=out.at[0, :, cols],
            send_sem=out_send.at[i, d],
            recv_sem=out_recv.at[i, d],
            device_id=(next_sec, peer(d)),
            device_id_type=MESH,
        )

    def out_arrived(i, d):
        source = lax.rem(a + groups - d, groups)
        cols = pl.ds(pl.multiple_of(source * width + i * dim, dim), dim)
        pltpu.make_async_remote_copy(
            src_ref=mixed.at[0, pl.ds(0, toks), :],
            dst_ref=out.at[0, :, cols],
            send_sem=out_send.at[i, d],
            recv_sem=out_recv.at[i, d],
            device_id=(next_sec, peer(d)),
            device_id_type=MESH,
        ).wait_recv()

    for i in range(heads):
        for d in range(2):
            back_arrived(0, i, d)
        total = partial_sum(0, i, 0) + back[0, i, 0].astype(F32) + back[0, i, 1].astype(F32)
        attention = (total[0:dim] / total[dim : dim + 1]).T
        attention = attention.astype(BF16).astype(F32)
        mixed[i] = (
            h_in[:, i * dim : (i + 1) * dim].astype(F32) + gate_row[i] * attention
        ).astype(BF16)
        for d in range(groups):
            out_copy(i, d).start()

    for kind in range(4):
        for d in range(1, groups):
            first_copy(kind, d).wait_send()

    def sent(i, carry):
        for r in range(reach):
            if r + 1 < reach:
                for d in range(2):
                    turn(r, i, d).wait_send()
            else:
                turn(r, i, far_way(i)).wait_send()
        for r in range(1, reach):
            for d in range(2):
                back_copy(r, i, d).wait_send()
        back_copy(reach, i, 0).wait_send()
        return carry

    lax.fori_loop(0, heads, sent, 0)
    for i in range(heads):
        for d in range(groups):
            out_copy(i, d).wait_send()
            out_arrived(i, d)


def shards(sections, fresh_qkv, stale_cache, norm_gains, hidden, gate_table, patch_index, step_index):
    seq_count = lax.axis_size("seq")
    groups = HEAD_GROUPS
    toks, full = hidden.shape[1:]
    width = full // groups
    heads = width // HEAD_DIM
    dim = HEAD_DIM
    block = toks * groups
    reach = seq_count // groups // 2
    patches, stale_rows = stale_cache.shape[2:4]
    key_count = (patches - 1) * stale_rows + block
    tall = dim + 16
    fresh = fresh_qkv.transpose(0, 2, 1, 3)
    anywhere = pl.BlockSpec(memory_space=pl.ANY)
    vmem = pl.BlockSpec(memory_space=pltpu.VMEM)
    smem = pl.BlockSpec(memory_space=pltpu.SMEM)
    dma = pltpu.SemaphoreType.DMA
    return pl.pallas_call(
        functools.partial(kernel, sections, seq_count),
        out_shape=jax.ShapeDtypeStruct(hidden.shape, BF16),
        in_specs=[anywhere, anywhere, vmem, anywhere, anywhere, smem, smem],
        out_specs=anywhere,
        scratch_shapes=[
            pltpu.VMEM((2, toks, full), BF16),
            pltpu.VMEM((patches, stale_rows, 2 * width), BF16),
            pltpu.VMEM(gate_table.shape[1:], BF16),
            pltpu.VMEM((heads, 1, dim), F32),
            pltpu.VMEM((groups, heads, toks, dim), BF16),
            pltpu.VMEM((groups, heads, toks, dim), BF16),
            pltpu.VMEM((reach, heads, 2, block, dim), BF16),
            pltpu.VMEM((heads, key_count, dim), BF16),
            pltpu.VMEM((heads, tall, key_count), BF16),
            pltpu.VMEM((block, width), BF16),
            pltpu.VMEM((block, width), BF16),
            pltpu.VMEM((reach, heads, tall, 2 * block), F32),
            pltpu.VMEM((reach, heads, 2, tall, block), BF16),
            pltpu.VMEM((reach, heads, 2, tall, block), BF16),
            pltpu.VMEM((heads, block, dim), BF16),
            dma((3,)),
            dma((2,)),
            dma((4, groups)),
            dma((4, groups)),
            dma((reach, heads, 2)),
            dma((reach + 1, heads, 2)),
            dma((reach + 1, heads, 2)),
            dma((reach, heads, 2)),
            dma((heads, groups)),
            dma((heads, groups)),
        ],
        compiler_params=pltpu.CompilerParams(
            collective_id=0, has_side_effects=True, vmem_limit_bytes=32 * 1024 * 1024
        ),
    )(fresh, stale_cache, norm_gains, hidden, gate_table, patch_index, step_index)


def solution(mesh):
    return jax.shard_map(
        functools.partial(shards, mesh.shape["section"]),
        mesh=mesh,
        in_specs=(
            P("section", "seq", None, None),
            P("section", "seq", None, None, None),
            P("section", None, None),
            P("section", "seq", None),
            P("section", None, None),
            P("section"),
            P("section"),
        ),
        out_specs=P("section", "seq", None),
        check_vma=False,
    )
```

```python
import functools

import jax
import jax.numpy as jnp
from jax import lax
from jax.experimental import pallas as pl
from jax.experimental.pallas import tpu as pltpu
from jax.sharding import PartitionSpec as P

HEADS = 24
HEAD_DIM = 128
HEAD_GROUPS = 8
SPACING = 4
MESH = pl.DeviceIdType.MESH
F32 = jnp.float32
BF16 = jnp.bfloat16


def slot_pair(r):
    if r == 0:
        return 0
    if r == SPACING:
        return 1
    return 2 * r if r > 0 else 1 - 2 * r


def kernel(
    sections,
    seq_count,
    fresh,
    stale,
    gains_in,
    hidden,
    gate,
    patch,
    step,
    out,
    raw,
    old,
    gains,
    gate_cols,
    gate_row,
    q_out,
    k_out,
    q_home,
    v_in,
    h_in,
    k_mine,
    v_mine,
    k_new,
    v_new,
    q_site,
    k_site,
    v_site,
    part,
    send,
    back,
    mixed,
    local_sem,
    first_send,
    first_recv,
    kv_send,
    kv_recv,
    q_send,
    q_recv,
    back_send,
    back_recv,
    out_send,
    out_recv,
):
    groups = HEAD_GROUPS
    ring = seq_count // groups
    heads = q_out.shape[1]
    toks = q_out.shape[2]
    dim = HEAD_DIM
    width = heads * dim
    block = groups * toks
    rows = old.shape[1]
    kept = old.shape[0] - 1
    stale_keys = kept * rows
    stale_at = (0, stale_keys, 2 * stale_keys, 3 * stale_keys, 3 * stale_keys + (kept - 1) * rows)
    fresh_base = 4 * stale_keys
    fresh_at = tuple(fresh_base + n * block for n in range(4))

    sec = lax.axis_index("section")
    me = lax.axis_index("seq")
    y = me // groups
    a = me % groups
    next_sec = lax.rem(sec + 1, sections)
    prev_sec = lax.rem(sec + sections - 1, sections)
    duty = lax.rem(y + SPACING - 2 * lax.rem(a, 2), SPACING)
    on_duty = duty < heads

    def peer(d):
        return y * groups + lax.rem(a + d, groups)

    def along(r):
        return lax.rem(y + ring + r, ring) * groups + a

    loads = [
        pltpu.make_async_copy(src, dst, local_sem.at[n])
        for n, (src, dst) in enumerate(
            (
                (gains_in.at[0], gains),
                (fresh.at[0, 0], raw.at[0]),
                (fresh.at[0, 1], raw.at[1]),
                (stale.at[0, 0], old),
            )
        )
    ]
    for load in loads:
        load.start()
    got_gains, got_q, got_k, got_old = loads

    barrier = pltpu.get_barrier_semaphore()
    for d in range(1, groups):
        pl.semaphore_signal(barrier, inc=1, device_id=(sec, peer(d)), device_id_type=MESH)
    for r in range(1, ring):
        pl.semaphore_signal(barrier, inc=1, device_id=(sec, along(r)), device_id_type=MESH)
    for d in range(groups):
        pl.semaphore_signal(barrier, inc=1, device_id=(prev_sec, peer(d)), device_id_type=MESH)

    mine = pl.ds(pl.multiple_of(a * toks, toks), toks)
    my_cols = pl.ds(pl.multiple_of(a * width, dim), width)
    late_loads = [
        pltpu.make_async_copy(src, dst, local_sem.at[len(loads) + n])
        for n, (src, dst) in enumerate(
            (
                (fresh.at[0, 2, :, my_cols], v_in.at[mine]),
                (hidden.at[0, :, my_cols], h_in.at[mine]),
                (gate.at[0, :, my_cols], gate_cols),
            )
        )
    ]
    for load in late_loads:
        load.start()

    def norm(which, stage):
        gain = gains[which : which + 1, :]
        for g in range(groups):
            for i in range(heads):
                col = (g * heads + i) * dim
                x = raw[which, :, col : col + dim].astype(F32)
                factor = lax.rsqrt(jnp.mean(x * x, axis=-1, keepdims=True) + 1e-06)
                stage[g, i] = (x * factor * gain).astype(BF16)

    got_gains.wait()
    got_q.wait()
    norm(0, q_out)
    q_home[:, mine, :] = q_out[a]

    pl.semaphore_wait(barrier, 2 * groups + ring - 2)

    def first_copy(kind, d):
        to = lax.rem(a + d, groups)
        cols = pl.ds(pl.multiple_of(to * width, dim), width)
        src, dst = (
            (lambda: q_out.at[to], lambda: q_home.at[:, mine, :]),
            (lambda: k_out.at[to], lambda: k_new.at[:, mine, :]),
            (lambda: fresh.at[0, 2, :, cols], lambda: v_in.at[mine]),
            (lambda: hidden.at[0, :, cols], lambda: h_in.at[mine]),
        )[kind]
        return pltpu.make_async_remote_copy(
            src_ref=src(),
            dst_ref=dst(),
            send_sem=first_send.at[kind, d],
            recv_sem=first_recv.at[kind, d],
            device_id=(sec, peer(d)),
            device_id_type=MESH,
        )

    def arrived(dst, sem):
        pltpu.make_async_remote_copy(
            src_ref=dst,
            dst_ref=dst,
            send_sem=first_send.at[0, 0],
            recv_sem=sem,
            device_id=(sec, peer(1)),
            device_id_type=MESH,
        ).wait_recv()

    def first_arrived(kind, d):
        source = lax.rem(a + groups - d, groups)
        spot = pl.ds(pl.multiple_of(source * toks, toks), toks)
        dst = (
            lambda: q_home.at[:, spot, :],
            lambda: k_new.at[:, spot, :],
            lambda: v_in.at[spot],
            lambda: h_in.at[spot],
        )[kind]()
        arrived(dst, first_recv.at[kind, d])

    for d in range(1, groups):
        first_copy(0, d).start()
    got_k.wait()
    norm(1, k_out)
    for kind in (1, 2):
        for d in range(1, groups):
            first_copy(kind, d).start()
    k_new[:, mine, :] = k_out[a]

    got_old.wait()
    skip = patch[0]
    for n in range(kept):
        m = n + (n >= skip).astype(jnp.int32)
        spot = slice(n * rows, (n + 1) * rows)
        for i in range(heads):
            k_mine[i, spot, :] = old[m, :, i * dim : (i + 1) * dim]
            v_mine[i, :, spot] = old[m, :, width + i * dim : width + (i + 1) * dim].T

    routes = (
        (1, 1, 0, kept, 1, True),
        (3, -1, 0, kept, 2, True),
        (2, 2, 0, kept - 1, 3, False),
        (2, -2, kept - 1, kept, 4, True),
    )
    fresh_number = {1: 1, 2: 2, 4: 3}

    def kv_copies(route, kinds):
        case, places, low, high, number, with_fresh = routes[route]
        i = lax.rem(duty + case, SPACING)
        count = (high - low) * rows
        spot, at = pl.ds(low * rows, count), pl.ds(stale_at[number], count)
        pairs = [
            (k_mine.at[i, spot, :], k_site.at[at, :]),
            (v_mine.at[i, :, spot], v_site.at[pl.ds(0, dim), at]),
        ]
        if with_fresh:
            at = pl.ds(fresh_at[fresh_number[number]], block)
            pairs += [
                (k_new.at[i], k_site.at[at, :]),
                (v_new.at[i], v_site.at[pl.ds(0, dim), at]),
            ]
        return [
            pltpu.make_async_remote_copy(
                src_ref=pairs[kind][0],
                dst_ref=pairs[kind][1],
                send_sem=kv_send.at[route, kind],
                recv_sem=kv_recv.at[route, kind],
                device_id=(sec, along(places)),
                device_id_type=MESH,
            )
            for kind in kinds
            if kind < len(pairs)
        ]

    def kv_start(kinds):
        for route in range(len(routes)):

            @pl.when(lax.rem(duty + routes[route][0], SPACING) < heads)
            def _(route=route):
                for copy in kv_copies(route, kinds):
                    copy.start()

    kv_start((0, 1))

    def q_copy(i, k):
        case = lax.rem(i - duty + SPACING, SPACING)
        places = case - k * SPACING
        if k == 0:
            slot = 2 * case + jnp.where(case == 0, 0, 1)
        else:
            slot = jnp.where(case == 0, 1, 2 * (SPACING - case))
        return case, pltpu.make_async_remote_copy(
            src_ref=q_home.at[i],
            dst_ref=q_site.at[slot],
            send_sem=q_send.at[i, k],
            recv_sem=q_recv.at[slot],
            device_id=(sec, along(places)),
            device_id_type=MESH,
        )

    for d in range(1, groups):
        first_arrived(0, d)
    for k in (1, 0):
        for i in range(heads):
            case, copy = q_copy(i, k)
            if k == 0:
                pl.when(case != 0)(copy.start)
            else:
                copy.start()

    for d in range(1, groups):
        first_copy(3, d).start()

    @pl.when(on_duty)
    def _():
        q_site[0] = q_home[duty]
        k_site[0:stale_keys, :] = k_mine[duty]
        v_site[0:dim, 0:stale_keys] = v_mine[duty]
        v_site[dim:, :] = jnp.ones_like(v_site[dim:, :])

    late_loads[0].wait()
    for kind in (1, 2):
        for d in range(1, groups):
            first_arrived(kind, d)
    for i in range(heads):
        v_new[i] = v_in[:, i * dim : (i + 1) * dim].T
    kv_start((2, 3))

    late_loads[2].wait()
    picked = lax.broadcasted_iota(jnp.int32, gate_cols.shape, 0) == step[0]
    gate_row[...] = jnp.sum(
        jnp.where(picked, gate_cols[...].astype(F32), 0.0), axis=0, keepdims=True
    )

    def attend(p, low, high):
        q = q_site[2 * p : 2 * p + 2].reshape(2 * block, dim)
        scores = lax.dot_general(
            k_site[low:high, :], q, (((1,), (1,)), ((), ())), preferred_element_type=F32
        )
        weights = jnp.exp(scores * (dim ** (-0.5))).astype(BF16)
        return jnp.dot(v_site[:, low:high], weights, preferred_element_type=F32)

    def back_copy(r):
        k = 0 if (-r) % ring < SPACING else 1
        return pltpu.make_async_remote_copy(
            src_ref=send.at[slot_pair(r)],
            dst_ref=back.at[duty, k],
            send_sem=back_send.at[slot_pair(r)],
            recv_sem=back_recv.at[duty, k],
            device_id=(sec, along(r)),
            device_id_type=MESH,
        )

    pairs = ((0, SPACING), (1, -1), (2, -2), (3, -3))

    @pl.when(on_duty)
    def _():
        for route in range(len(routes)):
            number, count = routes[route][4], (routes[route][3] - routes[route][2]) * rows
            at = pl.ds(stale_at[number], count)
            arrived(k_site.at[at, :], kv_recv.at[route, 0])
            arrived(v_site.at[pl.ds(0, dim), at], kv_recv.at[route, 1])
        for p in (1, 2, 3, 0):
            for r in pairs[p]:
                if r:
                    slot = slot_pair(r)
                    arrived(q_site.at[slot], q_recv.at[slot])
            part[p] = attend(p, 0, fresh_base)
        at = pl.ds(fresh_base, block)
        k_site[at, :] = k_new[duty]
        v_site[pl.ds(0, dim), at] = v_new[duty]
        for route in range(len(routes)):
            if routes[route][5]:
                at = pl.ds(fresh_at[fresh_number[routes[route][4]]], block)
                arrived(k_site.at[at, :], kv_recv.at[route, 2])
                arrived(v_site.at[pl.ds(0, dim), at], kv_recv.at[route, 3])
        for p in (0, 3, 2, 1):
            total = part[p] + attend(p, fresh_base, k_site.shape[0])
            for n, r in enumerate(pairs[p]):
                piece = total[:, n * block : (n + 1) * block].astype(BF16)
                if r == 0:
                    back[duty, 0] = piece
                else:
                    send[slot_pair(r)] = piece
                    back_copy(r).start()

    late_loads[1].wait()
    for d in range(1, groups):
        first_arrived(3, d)

    def out_copy(i, d):
        to = lax.rem(a + d, groups)
        spot = pl.ds(pl.multiple_of(to * toks, toks), toks)
        cols = pl.ds(pl.multiple_of(a * width + i * dim, dim), dim)
        return pltpu.make_async_remote_copy(
            src_ref=mixed.at[i, spot, :],
            dst_ref=out.at[0, :, cols],
            send_sem=out_send.at[i, d],
            recv_sem=out_recv.at[i, d],
            device_id=(next_sec, peer(d)),
            device_id_type=MESH,
        )

    for i in range(heads):
        case = lax.rem(i - duty + SPACING, SPACING)

        @pl.when(case != 0)
        def _(i=i):
            arrived(back.at[i, 0], back_recv.at[i, 0])

        arrived(back.at[i, 1], back_recv.at[i, 1])
        total = back[i, 0].astype(F32) + back[i, 1].astype(F32)
        attention = (total[0:dim] / total[dim : dim + 1]).T
        attention = attention.astype(BF16).astype(F32)
        cols = slice(i * dim, (i + 1) * dim)
        mixed[i] = (h_in[:, cols].astype(F32) + gate_row[:, cols] * attention).astype(BF16)
        for d in range(groups):
            out_copy(i, d).start()

    for kind in range(4):
        for d in range(1, groups):
            first_copy(kind, d).wait_send()
    for route in range(len(routes)):

        @pl.when(lax.rem(duty + routes[route][0], SPACING) < heads)
        def _(route=route):
            for copy in kv_copies(route, (0, 1, 2, 3)):
                copy.wait_send()

    for i in range(heads):
        for k in range(2):
            case, copy = q_copy(i, k)
            if k == 0:
                pl.when(case != 0)(copy.wait_send)
            else:
                copy.wait_send()

    @pl.when(on_duty)
    def _():
        for pair in pairs:
            for r in pair:
                if r:
                    back_copy(r).wait_send()

    for i in range(heads):
        for d in range(groups):
            out_copy(i, d).wait_send()
            source = lax.rem(a + groups - d, groups)
            cols = pl.ds(pl.multiple_of(source * width + i * dim, dim), dim)
            arrived(out.at[0, :, cols], out_recv.at[i, d])


def shards(sections, fresh_qkv, stale_cache, norm_gains, hidden, gate_table, patch_index, step_index):
    seq_count = lax.axis_size("seq")
    groups = HEAD_GROUPS
    ring = seq_count // groups
    toks, full = hidden.shape[1:]
    width = full // groups
    heads = width // HEAD_DIM
    dim = HEAD_DIM
    block = toks * groups
    patches, rows = stale_cache.shape[2:4]
    stale_keys = (patches - 1) * rows
    site_keys = 4 * (stale_keys + block)
    tall = dim + 16
    fresh = fresh_qkv.transpose(0, 2, 1, 3)
    hbm = pl.BlockSpec(memory_space=pltpu.HBM)
    smem = pl.BlockSpec(memory_space=pltpu.SMEM)
    dma = pltpu.SemaphoreType.DMA
    return pl.pallas_call(
        functools.partial(kernel, sections, seq_count),
        out_shape=jax.ShapeDtypeStruct(hidden.shape, BF16),
        in_specs=[hbm] * 5 + [smem] * 2,
        out_specs=pl.BlockSpec(memory_space=pl.ANY),
        scratch_shapes=[
            pltpu.VMEM((2, toks, full), BF16),
            pltpu.VMEM((patches, rows, 2 * width), BF16),
            pltpu.VMEM((2, dim), F32),
            pltpu.VMEM((gate_table.shape[1], width), BF16),
            pltpu.VMEM((1, width), F32),
            pltpu.VMEM((groups, heads, toks, dim), BF16),
            pltpu.VMEM((groups, heads, toks, dim), BF16),
            pltpu.VMEM((heads, block, dim), BF16),
            pltpu.VMEM((block, width), BF16),
            pltpu.VMEM((block, width), BF16),
            pltpu.VMEM((heads, stale_keys, dim), BF16),
            pltpu.VMEM((heads, dim, stale_keys), BF16),
            pltpu.VMEM((heads, block, dim), BF16),
            pltpu.VMEM((heads, dim, block), BF16),
            pltpu.VMEM((ring, block, dim), BF16),
            pltpu.VMEM((site_keys, dim), BF16),
            pltpu.VMEM((tall, site_keys), BF16),
            pltpu.VMEM((ring // 2, tall, 2 * block), F32),
            pltpu.VMEM((ring, tall, block), BF16),
            pltpu.VMEM((heads, 2, tall, block), BF16),
            pltpu.VMEM((heads, block, dim), BF16),
            dma((7,)),
            dma((4, groups)),
            dma((4, groups)),
            dma((4, 4)),
            dma((4, 4)),
            dma((heads, 2)),
            dma((ring,)),
            dma((ring,)),
            dma((heads, 2)),
            dma((heads, groups)),
            dma((heads, groups)),
        ],
        compiler_params=pltpu.CompilerParams(
            collective_id=0, has_side_effects=True, vmem_limit_bytes=24 * 1024 * 1024
        ),
    )(
        *(
            pltpu.with_memory_space_constraint(array, pltpu.HBM)
            for array in (
                fresh,
                stale_cache,
                norm_gains,
                hidden,
                gate_table,
            )
        ),
        patch_index,
        step_index,
    )


def solution(mesh):
    return jax.shard_map(
        functools.partial(shards, mesh.shape["section"]),
        mesh=mesh,
        in_specs=(
            P("section", "seq", None, None),
            P("section", "seq", None, None, None),
            P("section", None, None),
            P("section", "seq", None),
            P("section", None, None),
            P("section"),
            P("section"),
        ),
        out_specs=P("section", "seq", None),
        check_vma=False,
    )
```

```python
import functools

import jax
import jax.numpy as jnp
from jax import lax
from jax.experimental import pallas as pl
from jax.experimental.pallas import tpu as pltpu
from jax.sharding import PartitionSpec as P

HEADS = 24
HEAD_DIM = 128
HEAD_GROUPS = 8
SITES = 4
MESH = pl.DeviceIdType.MESH
F32 = jnp.float32
BF16 = jnp.bfloat16


def slot_of(r):
    if r == 0:
        return 0
    if r == SITES:
        return 1
    return 2 * r if r > 0 else 1 - 2 * r


PLACES = ((0, 2, -2, 4), (1, -1, 3, -3))


def kernel(
    sections,
    seq_count,
    fresh,
    stale,
    gains_in,
    hidden,
    gate,
    patch,
    step,
    out,
    raw,
    old,
    gains,
    gate_cols,
    gate_row,
    q_out,
    kv_out,
    q_home,
    h_in,
    k_mine,
    v_mine,
    q_site,
    k_site,
    v_site,
    kv_new,
    send,
    back,
    mixed,
    local_sem,
    first_send,
    first_recv,
    new_send,
    new_recv,
    kv_send,
    kv_recv,
    q_send,
    q_recv,
    back_send,
    back_recv,
    out_send,
    out_recv,
):
    groups = HEAD_GROUPS
    ring = seq_count // groups
    heads = q_out.shape[1]
    toks = q_out.shape[2]
    dim = HEAD_DIM
    width = heads * dim
    block = groups * toks
    rows = old.shape[1]
    kept = old.shape[0] - 1
    stale_keys = kept * rows
    last = (kept - 1) * rows
    before_at, after_at, fresh_at = stale_keys, stale_keys + last, 2 * stale_keys

    sec = lax.axis_index("section")
    me = lax.axis_index("seq")
    y = me // groups
    a = me % groups
    next_sec = lax.rem(sec + 1, sections)
    prev_sec = lax.rem(sec + sections - 1, sections)
    core = lax.rem(a, 2)
    parity = lax.rem(y, 2)

    def duty_of(parity, core):
        count = 1 + jnp.where(parity == core, 1, 0)
        return parity * (heads - count), count

    first_head, duty_count = duty_of(parity, core)

    def away(i, core=core):
        return lax.rem((i + core) // 2 + parity, 2)

    def flipped(d):
        bits = [1 << n for n in range(groups.bit_length() - 1)]
        return sum(
            bit * (1 - lax.rem(a // bit, 2) if d & bit else lax.rem(a // bit, 2)) for bit in bits
        )

    def along(r, d=0):
        return lax.rem(y + ring + r, ring) * groups + flipped(d)

    def peer(d):
        return along(0, d)

    pair, side = a // 2, a // (groups // 2)
    pieces = [
        pl.ds(pl.multiple_of(start * toks, toks), count * toks)
        for start, count in (
            (2 * pair, 2),
            (2 * (pair + 1 - 2 * lax.rem(pair, 2)), 2),
            ((1 - side) * (groups // 2), groups // 2),
        )
    ]

    barrier = pltpu.get_barrier_semaphore()

    def greet(section, seq):
        pl.semaphore_signal(barrier, inc=1, device_id=(section, seq), device_id_type=MESH)

    for d in range(groups - 1, 0, -1):
        greet(sec, along(0, d))
    for d in range(groups - 1, -1, -1):
        greet(sec, along(1, d))
    for r in (4, 3, -3, 2, -2, -1):
        greet(sec, along(r))
    greet(prev_sec, me)
    greeted = 2 * groups + 6

    mine = pl.ds(pl.multiple_of(a * toks, toks), toks)
    my_cols = pl.ds(pl.multiple_of(a * width, dim), width)
    loads = [
        pltpu.make_async_copy(src, dst, local_sem.at[n])
        for n, (src, dst) in enumerate(
            (
                (gains_in.at[0], gains),
                (fresh.at[0], raw),
                (stale.at[0, 0], old),
                (hidden.at[0, :, my_cols], h_in.at[mine]),
                (gate.at[0, :, my_cols], gate_cols),
            )
        )
    ]
    got_gains, got_raw, got_old, got_h, got_gate = loads
    for load in loads:
        load.start()

    def normed(which, g, i):
        col = (g * heads + i) * dim
        x = raw[which, :, col : col + dim].astype(F32)
        factor = lax.rsqrt(jnp.mean(x * x, axis=-1, keepdims=True) + 1e-06)
        return (x * factor * gains[which : which + 1, :]).astype(BF16)

    got_gains.wait()
    got_raw.wait()
    for g in range(groups):
        for i in range(heads):
            q_out[g, i] = normed(0, g, i)
    for g in range(groups):
        for i in range(heads):
            col = (g * heads + i) * dim
            kv_out[g, i, 0] = normed(1, g, i)
            kv_out[g, i, 1] = raw[2, :, col : col + dim]
    q_home[:, mine, :] = q_out[a]

    got_old.wait()
    skip = patch[0]
    for n in range(kept):
        m = n + (n >= skip).astype(jnp.int32)
        spot = slice(n * rows, (n + 1) * rows)
        for i in range(heads):
            k_mine[i, spot, :] = old[m, :, i * dim : (i + 1) * dim]
            v_mine[i, :, spot] = old[m, :, width + i * dim : width + (i + 1) * dim].T

    pl.semaphore_wait(barrier, greeted)

    def first_copy(kind, d):
        to = flipped(d)
        cols = pl.ds(pl.multiple_of(to * width, dim), width)
        src, dst = (
            (lambda: q_out.at[to], lambda: q_home.at[:, mine, :]),
            (lambda: hidden.at[0, :, cols], lambda: h_in.at[mine]),
        )[kind]
        return pltpu.make_async_remote_copy(
            src_ref=src(),
            dst_ref=dst(),
            send_sem=first_send.at[kind, d],
            recv_sem=first_recv.at[kind, d],
            device_id=(sec, peer(d)),
            device_id_type=MESH,
        )

    def arrived(dst, sem):
        pltpu.make_async_remote_copy(
            src_ref=dst,
            dst_ref=dst,
            send_sem=first_send.at[0, 0],
            recv_sem=sem,
            device_id=(sec, peer(1)),
            device_id_type=MESH,
        ).wait_recv()

    def first_arrived(kind, d):
        source = flipped(d)
        spot = pl.ds(pl.multiple_of(source * toks, toks), toks)
        dst = (lambda: q_home.at[:, spot, :], lambda: h_in.at[spot])[kind]()
        arrived(dst, first_recv.at[kind, d])

    def new_copy(d, off, count):
        to = flipped(d)
        first, _ = duty_of(lax.rem(parity + off, 2), lax.rem(to, 2))
        spot = pl.ds(pl.multiple_of(off * block + a * toks, toks), toks)
        return pltpu.make_async_remote_copy(
            src_ref=kv_out.at[to, pl.ds(first, count)],
            dst_ref=kv_new.at[pl.ds(0, count), :, spot, :],
            send_sem=new_send.at[d, off],
            recv_sem=new_recv.at[0],
            device_id=(sec, along(-off, d)),
            device_id_type=MESH,
        )

    def each_new(act):
        for d in range(groups):
            for off in range(2):
                if d or off:
                    for count in (1, 2):

                        @pl.when(duty_of(lax.rem(parity + off, 2), lax.rem(a + d, 2))[1] == count)
                        def _(d=d, off=off, count=count):
                            act(new_copy(d, off, count))

    for d in range(1, groups):
        first_copy(0, d).start()

    def stale_copies(i):
        there, _ = duty_of(1 - parity, core)
        j = i - there
        head, tail = pl.ds(0, last), pl.ds(last, rows)
        head_at, tail_at = pl.ds(before_at, last), pl.ds(after_at, rows)
        deep = pl.ds(0, dim)
        return [
            pltpu.make_async_remote_copy(
                src_ref=src,
                dst_ref=dst,
                send_sem=kv_send.at[i, n],
                recv_sem=kv_recv.at[j, n],
                device_id=(sec, along(places)),
                device_id_type=MESH,
            )
            for n, (src, dst, places) in enumerate(
                (
                    (k_mine.at[i, head, :], k_site.at[j, head_at, :], 1),
                    (v_mine.at[i, :, head], v_site.at[j, deep, head_at], 1),
                    (k_mine.at[i, tail, :], k_site.at[j, tail_at, :], -1),
                    (v_mine.at[i, :, tail], v_site.at[j, deep, tail_at], -1),
                )
            )
        ]

    for i in range(heads):

        @pl.when(away(i) == 1)
        def _(i=i):
            for copy in stale_copies(i):
                copy.start()

    def own_part(j, carry):
        k_site[j, 0:stale_keys, :] = k_mine[first_head + j]
        v_site[j, 0:dim, 0:stale_keys] = v_mine[first_head + j]
        v_site[j, dim:, :] = jnp.ones_like(v_site[j, dim:, :])
        kv_new[j, :, mine, :] = kv_out[a, first_head + j]
        return carry

    lax.fori_loop(0, duty_count, own_part, 0)
    each_new(lambda copy: copy.start())

    def q_copy(i, off, k, piece):
        places = PLACES[off][k]
        there, _ = duty_of(lax.rem(parity + off, 2), core)
        j, slot = i - there, slot_of(SITES if places == SITES else -places)
        return pltpu.make_async_remote_copy(
            src_ref=q_home.at[i, pieces[piece], :],
            dst_ref=q_site.at[j, slot, pieces[piece], :],
            send_sem=q_send.at[i, k, piece],
            recv_sem=q_recv.at[j, slot, piece],
            device_id=(sec, along(places)),
            device_id_type=MESH,
        )

    def each_q(piece, act):
        for k in (3, 2, 1, 0):
            for i in range(heads):
                for off in range(2):
                    if PLACES[off][k]:

                        @pl.when(away(i) == off)
                        def _(i=i, off=off, k=k):
                            act(q_copy(i, off, k, piece))

    for piece, low, high in ((0, 1, 2), (1, 2, 4), (2, 4, groups)):
        for d in range(low, high):
            first_arrived(0, d)
        each_q(piece, lambda copy: copy.start())

    for d in range(1, groups):
        first_copy(1, d).start()

    def own_block(j, carry):
        q_site[j, 0] = q_home[first_head + j]
        return carry

    lax.fori_loop(0, duty_count, own_block, 0)

    got_gate.wait()
    picked = lax.broadcasted_iota(jnp.int32, gate_cols.shape, 0) == step[0]
    gate_row[...] = jnp.sum(
        jnp.where(picked, gate_cols[...].astype(F32), 0.0), axis=0, keepdims=True
    )

    def attend(p, j):
        q = q_site[j, 2 * p : 2 * p + 2].reshape(2 * block, dim)
        scores = lax.dot_general(
            k_site[j], q, (((1,), (1,)), ((), ())), preferred_element_type=F32
        )
        weights = jnp.exp(scores * (dim ** (-0.5))).astype(BF16)
        return jnp.dot(v_site[j], weights, preferred_element_type=F32)

    def back_copy(j, r):
        k = PLACES[r % 2].index(r if r == SITES else -r)
        return pltpu.make_async_remote_copy(
            src_ref=send.at[j, slot_of(r)],
            dst_ref=back.at[first_head + j, k],
            send_sem=back_send.at[j, slot_of(r)],
            recv_sem=back_recv.at[first_head + j, k],
            device_id=(sec, along(r)),
            device_id_type=MESH,
        )

    pairs = ((0, SITES), (1, -1), (2, -2), (3, -3))

    def keys_here(j, carry):
        head_at, tail_at = pl.ds(before_at, last), pl.ds(after_at, rows)
        arrived(k_site.at[j, head_at, :], kv_recv.at[j, 0])
        arrived(v_site.at[j, pl.ds(0, dim), head_at], kv_recv.at[j, 1])
        arrived(k_site.at[j, tail_at, :], kv_recv.at[j, 2])
        arrived(v_site.at[j, pl.ds(0, dim), tail_at], kv_recv.at[j, 3])
        return carry

    lax.fori_loop(0, duty_count, keys_here, 0)
    for count in (1, 2):

        @pl.when(duty_count == count)
        def _(count=count):
            arrived(kv_new.at[0:count, :, 0 : 2 * block - toks, :], new_recv.at[0])

    def fresh_here(j, carry):
        k_site[j, fresh_at:, :] = kv_new[j, 0]
        for n in range(2):
            spot = slice(n * block, (n + 1) * block)
            at = slice(fresh_at + n * block, fresh_at + (n + 1) * block)
            v_site[j, 0:dim, at] = kv_new[j, 1, spot, :].T
        return carry

    lax.fori_loop(0, duty_count, fresh_here, 0)

    for p in (0, 3, 2, 1):

        def work(j, carry, p=p):
            for r in pairs[p]:
                if r:
                    slot = slot_of(r)
                    for piece, spot in enumerate(pieces):
                        arrived(q_site.at[j, slot, spot, :], q_recv.at[j, slot, piece])
            total = attend(p, j)
            for n, r in enumerate(pairs[p]):
                piece = total[:, n * block : (n + 1) * block].astype(BF16)
                if r == 0:
                    back[first_head + j, 0] = piece
                else:
                    send[j, slot_of(r)] = piece
                    back_copy(j, r).start()
            return carry

        lax.fori_loop(0, duty_count, work, 0)

    got_h.wait()
    for d in range(1, groups):
        first_arrived(1, d)

    def out_copy(i, d):
        to = flipped(d)
        spot = pl.ds(pl.multiple_of(to * toks, toks), toks)
        cols = pl.ds(pl.multiple_of(a * width + i * dim, dim), dim)
        return pltpu.make_async_remote_copy(
            src_ref=mixed.at[i, spot, :],
            dst_ref=out.at[0, :, cols],
            send_sem=out_send.at[i, d],
            recv_sem=out_recv.at[0],
            device_id=(next_sec, peer(d)),
            device_id_type=MESH,
        )

    for i in range(heads):
        pl.when(away(i) == 1)(lambda i=i: arrived(back.at[i, 0], back_recv.at[i, 0]))
        for k in range(1, SITES):
            arrived(back.at[i, k], back_recv.at[i, k])
        total = sum(back[i, k].astype(F32) for k in range(SITES))
        attention = (total[0:dim] / total[dim : dim + 1]).T
        attention = attention.astype(BF16).astype(F32)
        cols = slice(i * dim, (i + 1) * dim)
        mixed[i] = (h_in[:, cols].astype(F32) + gate_row[:, cols] * attention).astype(BF16)
        for d in range(groups):
            out_copy(i, d).start()

    for kind in range(2):
        for d in range(1, groups):
            first_copy(kind, d).wait_send()
    each_new(lambda copy: copy.wait_send())
    for i in range(heads):

        @pl.when(away(i) == 1)
        def _(i=i):
            for copy in stale_copies(i):
                copy.wait_send()

    for piece in range(3):
        each_q(piece, lambda copy: copy.wait_send())

    def backs_sent(j, carry):
        for pair in pairs:
            for r in pair:
                if r:
                    back_copy(j, r).wait_send()
        return carry

    lax.fori_loop(0, duty_count, backs_sent, 0)
    for i in range(heads):
        for d in range(groups):
            out_copy(i, d).wait_send()
    arrived(out, out_recv.at[0])


def shards(sections, fresh_qkv, stale_cache, norm_gains, hidden, gate_table, patch_index, step_index):
    seq_count = lax.axis_size("seq")
    groups = HEAD_GROUPS
    ring = seq_count // groups
    toks, full = hidden.shape[1:]
    width = full // groups
    heads = width // HEAD_DIM
    dim = HEAD_DIM
    block = toks * groups
    patches, rows = stale_cache.shape[2:4]
    stale_keys = (patches - 1) * rows
    tall = dim + 16
    fresh = fresh_qkv.transpose(0, 2, 1, 3)
    hbm = pl.BlockSpec(memory_space=pltpu.HBM)
    smem = pl.BlockSpec(memory_space=pltpu.SMEM)
    dma = pltpu.SemaphoreType.DMA
    return pl.pallas_call(
        functools.partial(kernel, sections, seq_count),
        out_shape=jax.ShapeDtypeStruct(hidden.shape, BF16),
        in_specs=[hbm] * 5 + [smem] * 2,
        out_specs=pl.BlockSpec(memory_space=pl.ANY),
        scratch_shapes=[
            pltpu.VMEM((3, toks, full), BF16),
            pltpu.VMEM((patches, rows, 2 * width), BF16),
            pltpu.VMEM((2, dim), F32),
            pltpu.VMEM((gate_table.shape[1], width), BF16),
            pltpu.VMEM((1, width), F32),
            pltpu.VMEM((groups, heads, toks, dim), BF16),
            pltpu.VMEM((groups, heads, 2, toks, dim), BF16),
            pltpu.VMEM((heads, block, dim), BF16),
            pltpu.VMEM((block, width), BF16),
            pltpu.VMEM((heads, stale_keys, dim), BF16),
            pltpu.VMEM((heads, dim, stale_keys), BF16),
            pltpu.VMEM((2, ring, block, dim), BF16),
            pltpu.VMEM((2, 2 * (stale_keys + block), dim), BF16),
            pltpu.VMEM((2, tall, 2 * (stale_keys + block)), BF16),
            pltpu.VMEM((2, 2, 2 * block, dim), BF16),
            pltpu.VMEM((2, ring, tall, block), BF16),
            pltpu.VMEM((heads, SITES, tall, block), BF16),
            pltpu.VMEM((heads, block, dim), BF16),
            dma((5,)),
            dma((2, groups)),
            dma((2, groups)),
            dma((groups, 2)),
            dma((1,)),
            dma((heads, 4)),
            dma((2, 4)),
            dma((heads, SITES, 3)),
            dma((2, ring, 3)),
            dma((2, ring)),
            dma((heads, SITES)),
            dma((heads, groups)),
            dma((1,)),
        ],
        compiler_params=pltpu.CompilerParams(
            collective_id=0, has_side_effects=True, vmem_limit_bytes=24 * 1024 * 1024
        ),
    )(
        *(
            pltpu.with_memory_space_constraint(array, pltpu.HBM)
            for array in (
                fresh,
                stale_cache,
                norm_gains,
                hidden,
                gate_table,
            )
        ),
        patch_index,
        step_index,
    )


def solution(mesh):
    return jax.shard_map(
        functools.partial(shards, mesh.shape["section"]),
        mesh=mesh,
        in_specs=(
            P("section", "seq", None, None),
            P("section", "seq", None, None, None),
            P("section", None, None),
            P("section", "seq", None),
            P("section", None, None),
            P("section"),
            P("section"),
        ),
        out_specs=P("section", "seq", None),
        check_vma=False,
    )
```

```python
import functools

import jax
import jax.numpy as jnp
from jax import lax
from jax.experimental import pallas as pl
from jax.experimental.pallas import tpu as pltpu
from jax.sharding import PartitionSpec as P

HEADS = 24
HEAD_DIM = 128
HEAD_GROUPS = 8
SITES = 4
MESH = pl.DeviceIdType.MESH
F32 = jnp.float32
BF16 = jnp.bfloat16


def slot_of(r):
    if r == 0:
        return 0
    if r == SITES:
        return 1
    return 2 * r if r > 0 else 1 - 2 * r


PLACES = ((0, 2, -2, 4), (1, -1, 3, -3))


def kernel(
    sections,
    seq_count,
    fresh,
    stale,
    gains_in,
    hidden,
    gate,
    patch,
    step,
    out,
    raw,
    old,
    gains,
    gate_cols,
    gate_row,
    q_out,
    kv_out,
    q_home,
    h_in,
    k_mine,
    v_mine,
    q_site,
    k_site,
    v_site,
    kv_new,
    part,
    send,
    mid,
    back,
    mixed,
    local_sem,
    first_send,
    first_recv,
    new_send,
    new_recv,
    kv_send,
    kv_recv,
    q_send,
    q_recv,
    back_send,
    back_recv,
    mid_send,
    mid_recv,
    out_send,
    out_recv,
):
    groups = HEAD_GROUPS
    ring = seq_count // groups
    heads = q_out.shape[1]
    toks = q_out.shape[2]
    dim = HEAD_DIM
    width = heads * dim
    block = groups * toks
    rows = old.shape[1]
    kept = old.shape[0] - 1
    tall = send.shape[2]
    stale_keys = kept * rows
    last = (kept - 1) * rows
    before_at, after_at, fresh_at = stale_keys, stale_keys + last, 2 * stale_keys

    sec = lax.axis_index("section")
    me = lax.axis_index("seq")
    y = me // groups
    a = me % groups
    next_sec = lax.rem(sec + 1, sections)
    prev_sec = lax.rem(sec + sections - 1, sections)
    core = lax.rem(a, 2)
    parity = lax.rem(y, 2)

    def duty_of(parity, core):
        count = 1 + jnp.where(parity == core, 1, 0)
        return parity * (heads - count), count

    first_head, duty_count = duty_of(parity, core)

    def away(i, core=core):
        return lax.rem((i + core) // 2 + parity, 2)

    def flipped(d):
        bits = [1 << n for n in range(groups.bit_length() - 1)]
        return sum(
            bit * (1 - lax.rem(a // bit, 2) if d & bit else lax.rem(a // bit, 2)) for bit in bits
        )

    def along(r, d=0):
        return lax.rem(y + ring + r, ring) * groups + flipped(d)

    def peer(d):
        return along(0, d)

    pair, side = a // 2, a // (groups // 2)
    pieces = [
        pl.ds(pl.multiple_of(start * toks, toks), count * toks)
        for start, count in (
            (2 * pair, 2),
            (2 * (pair + 1 - 2 * lax.rem(pair, 2)), 2),
            ((1 - side) * (groups // 2), groups // 2),
        )
    ]

    barrier = pltpu.get_barrier_semaphore()

    def greet(section, seq):
        pl.semaphore_signal(barrier, inc=1, device_id=(section, seq), device_id_type=MESH)

    for d in range(groups - 1, 0, -1):
        greet(sec, along(0, d))
    for d in range(groups - 1, -1, -1):
        greet(sec, along(1, d))
    for r in (4, 3, -3, 2, -2, -1):
        greet(sec, along(r))
    greet(prev_sec, me)
    greeted = 2 * groups + 6

    mine = pl.ds(pl.multiple_of(a * toks, toks), toks)
    my_cols = pl.ds(pl.multiple_of(a * width, dim), width)
    loads = [
        pltpu.make_async_copy(src, dst, local_sem.at[n])
        for n, (src, dst) in enumerate(
            (
                (gains_in.at[0], gains),
                (fresh.at[0], raw),
                (stale.at[0, 0], old),
                (hidden.at[0, :, my_cols], h_in.at[mine]),
                (gate.at[0, :, my_cols], gate_cols),
            )
        )
    ]
    got_gains, got_raw, got_old, got_h, got_gate = loads
    for load in loads:
        load.start()

    def normed(which, g, i):
        col = (g * heads + i) * dim
        x = raw[which, :, col : col + dim].astype(F32)
        factor = lax.rsqrt(jnp.mean(x * x, axis=-1, keepdims=True) + 1e-06)
        return (x * factor * gains[which : which + 1, :]).astype(BF16)

    got_gains.wait()
    got_raw.wait()
    for g in range(groups):
        for i in range(heads):
            q_out[g, i] = normed(0, g, i)
    for g in range(groups):
        for i in range(heads):
            col = (g * heads + i) * dim
            kv_out[g, i, 0] = normed(1, g, i)
            kv_out[g, i, 1] = raw[2, :, col : col + dim]
    q_home[:, mine, :] = q_out[a]

    got_old.wait()
    skip = patch[0]
    for n in range(kept):
        m = n + (n >= skip).astype(jnp.int32)
        spot = slice(n * rows, (n + 1) * rows)
        for i in range(heads):
            k_mine[i, spot, :] = old[m, :, i * dim : (i + 1) * dim]
            v_mine[i, :, spot] = old[m, :, width + i * dim : width + (i + 1) * dim].T

    pl.semaphore_wait(barrier, greeted)

    def first_copy(kind, d):
        to = flipped(d)
        cols = pl.ds(pl.multiple_of(to * width, dim), width)
        src, dst = (
            (lambda: q_out.at[to], lambda: q_home.at[:, mine, :]),
            (lambda: hidden.at[0, :, cols], lambda: h_in.at[mine]),
        )[kind]
        return pltpu.make_async_remote_copy(
            src_ref=src(),
            dst_ref=dst(),
            send_sem=first_send.at[kind, d],
            recv_sem=first_recv.at[kind, d],
            device_id=(sec, peer(d)),
            device_id_type=MESH,
        )

    def arrived(dst, sem):
        pltpu.make_async_remote_copy(
            src_ref=dst,
            dst_ref=dst,
            send_sem=first_send.at[0, 0],
            recv_sem=sem,
            device_id=(sec, peer(1)),
            device_id_type=MESH,
        ).wait_recv()

    def first_arrived(kind, d):
        source = flipped(d)
        spot = pl.ds(pl.multiple_of(source * toks, toks), toks)
        dst = (lambda: q_home.at[:, spot, :], lambda: h_in.at[spot])[kind]()
        arrived(dst, first_recv.at[kind, d])

    def new_copy(d, off, count):
        to = flipped(d)
        first, _ = duty_of(lax.rem(parity + off, 2), lax.rem(to, 2))
        spot = pl.ds(pl.multiple_of(off * block + a * toks, toks), toks)
        return pltpu.make_async_remote_copy(
            src_ref=kv_out.at[to, pl.ds(first, count)],
            dst_ref=kv_new.at[pl.ds(0, count), :, spot, :],
            send_sem=new_send.at[d, off],
            recv_sem=new_recv.at[0],
            device_id=(sec, along(-off, d)),
            device_id_type=MESH,
        )

    def each_new(act):
        for d in range(groups):
            for off in range(2):
                if d or off:
                    for count in (1, 2):

                        @pl.when(duty_of(lax.rem(parity + off, 2), lax.rem(a + d, 2))[1] == count)
                        def _(d=d, off=off, count=count):
                            act(new_copy(d, off, count))

    for d in range(1, groups):
        first_copy(0, d).start()

    def stale_copies(i):
        there, _ = duty_of(1 - parity, core)
        j = i - there
        head, tail = pl.ds(0, last), pl.ds(last, rows)
        head_at, tail_at = pl.ds(before_at, last), pl.ds(after_at, rows)
        deep = pl.ds(0, dim)
        return [
            pltpu.make_async_remote_copy(
                src_ref=src,
                dst_ref=dst,
                send_sem=kv_send.at[i, n],
                recv_sem=kv_recv.at[j, n],
                device_id=(sec, along(places)),
                device_id_type=MESH,
            )
            for n, (src, dst, places) in enumerate(
                (
                    (k_mine.at[i, head, :], k_site.at[j, head_at, :], 1),
                    (v_mine.at[i, :, head], v_site.at[j, deep, head_at], 1),
                    (k_mine.at[i, tail, :], k_site.at[j, tail_at, :], -1),
                    (v_mine.at[i, :, tail], v_site.at[j, deep, tail_at], -1),
                )
            )
        ]

    for i in range(heads):

        @pl.when(away(i) == 1)
        def _(i=i):
            for copy in stale_copies(i):
                copy.start()
            back[i, 2] = jnp.zeros_like(back[i, 2])

    def own_part(j, carry):
        k_site[j, 0:stale_keys, :] = k_mine[first_head + j]
        v_site[j, 0:dim, 0:stale_keys] = v_mine[first_head + j]
        v_site[j, dim:, :] = jnp.ones_like(v_site[j, dim:, :])
        kv_new[j, :, mine, :] = kv_out[a, first_head + j]
        return carry

    lax.fori_loop(0, duty_count, own_part, 0)
    each_new(lambda copy: copy.start())

    def q_copy(i, off, k, piece):
        places = PLACES[off][k]
        there, _ = duty_of(lax.rem(parity + off, 2), core)
        j, slot = i - there, slot_of(SITES if places == SITES else -places)
        return pltpu.make_async_remote_copy(
            src_ref=q_home.at[i, pieces[piece], :],
            dst_ref=q_site.at[j, slot, pieces[piece], :],
            send_sem=q_send.at[i, k, piece],
            recv_sem=q_recv.at[j, slot, piece],
            device_id=(sec, along(places)),
            device_id_type=MESH,
        )

    def each_q(piece, act, order=(3, 2, 1, 0)):
        for k in order:
            for i in range(heads):
                for off in range(2):
                    if PLACES[off][k]:

                        @pl.when(away(i) == off)
                        def _(i=i, off=off, k=k):
                            act(q_copy(i, off, k, piece))

    for piece, low, high in ((0, 1, 2), (1, 2, 4), (2, 4, groups)):
        for d in range(low, high):
            first_arrived(0, d)
        each_q(piece, lambda copy: copy.start(), (3, 2) if piece else (3, 2, 1, 0))
    for piece in (1, 2):
        each_q(piece, lambda copy: copy.start(), (1, 0))
    for d in range(1, groups):
        first_copy(1, d).start()

    def own_block(j, carry):
        q_site[j, 0] = q_home[first_head + j]
        return carry

    lax.fori_loop(0, duty_count, own_block, 0)

    got_gate.wait()
    picked = lax.broadcasted_iota(jnp.int32, gate_cols.shape, 0) == step[0]
    gate_row[...] = jnp.sum(
        jnp.where(picked, gate_cols[...].astype(F32), 0.0), axis=0, keepdims=True
    )

    def attend(p, j):
        q = q_site[j, 2 * p : 2 * p + 2].reshape(2 * block, dim)
        scores = lax.dot_general(
            k_site[j], q, (((1,), (1,)), ((), ())), preferred_element_type=F32
        )
        weights = jnp.exp(scores * (dim ** (-0.5))).astype(BF16)
        return jnp.dot(v_site[j], weights, preferred_element_type=F32)

    near = (2, -2, 1, -1)
    cut = dim // 2

    def back_copy(j, r):
        k = PLACES[r % 2].index(-r)
        return pltpu.make_async_remote_copy(
            src_ref=send.at[j, slot_of(r)],
            dst_ref=back.at[first_head + j, k],
            send_sem=back_send.at[j, slot_of(r)],
            recv_sem=back_recv.at[first_head + j, k],
            device_id=(sec, along(r)),
            device_id_type=MESH,
        )

    hops = (
        (SITES, 2, 2, pl.ds(0, cut)),
        (SITES, -2, -2, pl.ds(cut, tall - cut)),
        (3, 2, 1, pl.ds(0, tall)),
        (-3, -2, -1, pl.ds(0, tall)),
    )

    def mid_copy(j, hop):
        r, way, there, spot = hops[hop]
        return pltpu.make_async_remote_copy(
            src_ref=send.at[j, slot_of(r), spot, :],
            dst_ref=mid.at[j, hop, spot, :],
            send_sem=mid_send.at[j, hop],
            recv_sem=mid_recv.at[j, hop],
            device_id=(sec, along(way)),
            device_id_type=MESH,
        )

    pairs = ((0, SITES), (1, -1), (2, -2), (3, -3))

    def keys_here(j, carry):
        head_at, tail_at = pl.ds(before_at, last), pl.ds(after_at, rows)
        arrived(k_site.at[j, head_at, :], kv_recv.at[j, 0])
        arrived(v_site.at[j, pl.ds(0, dim), head_at], kv_recv.at[j, 1])
        arrived(k_site.at[j, tail_at, :], kv_recv.at[j, 2])
        arrived(v_site.at[j, pl.ds(0, dim), tail_at], kv_recv.at[j, 3])
        return carry

    lax.fori_loop(0, duty_count, keys_here, 0)
    for count in (1, 2):

        @pl.when(duty_count == count)
        def _(count=count):
            arrived(kv_new.at[0:count, :, 0 : 2 * block - toks, :], new_recv.at[0])

    def fresh_here(j, carry):
        k_site[j, fresh_at:, :] = kv_new[j, 0]
        for n in range(2):
            spot = slice(n * block, (n + 1) * block)
            at = slice(fresh_at + n * block, fresh_at + (n + 1) * block)
            v_site[j, 0:dim, at] = kv_new[j, 1, spot, :].T
        return carry

    lax.fori_loop(0, duty_count, fresh_here, 0)

    for p in (0, 3, 2, 1):

        def work(j, carry, p=p):
            for r in pairs[p]:
                if r:
                    slot = slot_of(r)
                    for piece, spot in enumerate(pieces):
                        arrived(q_site.at[j, slot, spot, :], q_recv.at[j, slot, piece])
            total = attend(p, j)
            for n, r in enumerate(pairs[p]):
                sums = total[:, n * block : (n + 1) * block]
                if r == 0:
                    back[first_head + j, 0] = sums.astype(BF16)
                elif r in near:
                    part[j, near.index(r)] = sums
                else:
                    send[j, slot_of(r)] = sums.astype(BF16)
                    for hop in range(len(hops)):
                        if hops[hop][0] == r:
                            mid_copy(j, hop).start()
            return carry

        lax.fori_loop(0, duty_count, work, 0)

    for hop, (_, _, r, spot) in enumerate(hops):

        def add_on(j, carry, hop=hop, r=r, spot=spot):
            arrived(mid.at[j, hop, spot, :], mid_recv.at[j, hop])
            n = near.index(r)
            sums = part[j, n, spot, :] + mid[j, hop, spot, :].astype(F32)
            send[j, slot_of(r), spot, :] = sums.astype(BF16)
            if r == 2:
                send[j, slot_of(r), cut:, :] = part[j, n, cut:, :].astype(BF16)
            if r == -2:
                send[j, slot_of(r), 0:cut, :] = part[j, n, 0:cut, :].astype(BF16)
            back_copy(j, r).start()
            return carry

        lax.fori_loop(0, duty_count, add_on, 0)

    got_h.wait()
    for d in range(1, groups):
        first_arrived(1, d)

    def out_copy(i, d):
        to = flipped(d)
        spot = pl.ds(pl.multiple_of(to * toks, toks), toks)
        cols = pl.ds(pl.multiple_of(a * width + i * dim, dim), dim)
        return pltpu.make_async_remote_copy(
            src_ref=mixed.at[i, spot, :],
            dst_ref=out.at[0, :, cols],
            send_sem=out_send.at[i, d],
            recv_sem=out_recv.at[0],
            device_id=(next_sec, peer(d)),
            device_id_type=MESH,
        )

    for i in range(heads):
        pl.when(away(i) == 1)(lambda i=i: arrived(back.at[i, 0], back_recv.at[i, 0]))
        arrived(back.at[i, 1], back_recv.at[i, 1])
        pl.when(away(i) == 0)(lambda i=i: arrived(back.at[i, 2], back_recv.at[i, 2]))
        total = sum(back[i, k].astype(F32) for k in range(3))
        attention = (total[0:dim] / total[dim : dim + 1]).T
        attention = attention.astype(BF16).astype(F32)
        cols = slice(i * dim, (i + 1) * dim)
        mixed[i] = (h_in[:, cols].astype(F32) + gate_row[:, cols] * attention).astype(BF16)
        for d in range(groups):
            out_copy(i, d).start()

    for kind in range(2):
        for d in range(1, groups):
            first_copy(kind, d).wait_send()
    each_new(lambda copy: copy.wait_send())
    for i in range(heads):

        @pl.when(away(i) == 1)
        def _(i=i):
            for copy in stale_copies(i):
                copy.wait_send()

    for piece in range(3):
        each_q(piece, lambda copy: copy.wait_send())

    def backs_sent(j, carry):
        for n in range(4):
            back_copy(j, near[n]).wait_send()
            mid_copy(j, n).wait_send()
        return carry

    lax.fori_loop(0, duty_count, backs_sent, 0)
    for i in range(heads):
        for d in range(groups):
            out_copy(i, d).wait_send()
    arrived(out, out_recv.at[0])


def shards(sections, fresh_qkv, stale_cache, norm_gains, hidden, gate_table, patch_index, step_index):
    seq_count = lax.axis_size("seq")
    groups = HEAD_GROUPS
    ring = seq_count // groups
    toks, full = hidden.shape[1:]
    width = full // groups
    heads = width // HEAD_DIM
    dim = HEAD_DIM
    block = toks * groups
    patches, rows = stale_cache.shape[2:4]
    stale_keys = (patches - 1) * rows
    tall = dim + 16
    fresh = fresh_qkv.transpose(0, 2, 1, 3)
    hbm = pl.BlockSpec(memory_space=pltpu.HBM)
    smem = pl.BlockSpec(memory_space=pltpu.SMEM)
    dma = pltpu.SemaphoreType.DMA
    return pl.pallas_call(
        functools.partial(kernel, sections, seq_count),
        out_shape=jax.ShapeDtypeStruct(hidden.shape, BF16),
        in_specs=[hbm] * 5 + [smem] * 2,
        out_specs=pl.BlockSpec(memory_space=pl.ANY),
        scratch_shapes=[
            pltpu.VMEM((3, toks, full), BF16),
            pltpu.VMEM((patches, rows, 2 * width), BF16),
            pltpu.VMEM((2, dim), F32),
            pltpu.VMEM((gate_table.shape[1], width), BF16),
            pltpu.VMEM((1, width), F32),
            pltpu.VMEM((groups, heads, toks, dim), BF16),
            pltpu.VMEM((groups, heads, 2, toks, dim), BF16),
            pltpu.VMEM((heads, block, dim), BF16),
            pltpu.VMEM((block, width), BF16),
            pltpu.VMEM((heads, stale_keys, dim), BF16),
            pltpu.VMEM((heads, dim, stale_keys), BF16),
            pltpu.VMEM((2, ring, block, dim), BF16),
            pltpu.VMEM((2, 2 * (stale_keys + block), dim), BF16),
            pltpu.VMEM((2, tall, 2 * (stale_keys + block)), BF16),
            pltpu.VMEM((2, 2, 2 * block, dim), BF16),
            pltpu.VMEM((2, 4, tall, block), F32),
            pltpu.VMEM((2, ring, tall, block), BF16),
            pltpu.VMEM((2, 4, tall, block), BF16),
            pltpu.VMEM((heads, 3, tall, block), BF16),
            pltpu.VMEM((heads, block, dim), BF16),
            dma((5,)),
            dma((2, groups)),
            dma((2, groups)),
            dma((groups, 2)),
            dma((1,)),
            dma((heads, 4)),
            dma((2, 4)),
            dma((heads, SITES, 3)),
            dma((2, ring, 3)),
            dma((2, ring)),
            dma((heads, 3)),
            dma((2, 4)),
            dma((2, 4)),
            dma((heads, groups)),
            dma((1,)),
        ],
        compiler_params=pltpu.CompilerParams(
            collective_id=0, has_side_effects=True, vmem_limit_bytes=24 * 1024 * 1024
        ),
    )(
        *(
            pltpu.with_memory_space_constraint(array, pltpu.HBM)
            for array in (
                fresh,
                stale_cache,
                norm_gains,
                hidden,
                gate_table,
            )
        ),
        patch_index,
        step_index,
    )


def solution(mesh):
    return jax.shard_map(
        functools.partial(shards, mesh.shape["section"]),
        mesh=mesh,
        in_specs=(
            P("section", "seq", None, None),
            P("section", "seq", None, None, None),
            P("section", None, None),
            P("section", "seq", None),
            P("section", None, None),
            P("section"),
            P("section"),
        ),
        out_specs=P("section", "seq", None),
        check_vma=False,
    )
```

```python
import functools

import jax
import jax.numpy as jnp
from jax import lax
from jax.experimental import pallas as pl
from jax.experimental.pallas import tpu as pltpu
from jax.sharding import PartitionSpec as P

HEADS = 24
HEAD_DIM = 128
HEAD_GROUPS = 8
SITES = 4
MESH = pl.DeviceIdType.MESH
F32 = jnp.float32
BF16 = jnp.bfloat16


def slot_of(r):
    if r == 0:
        return 0
    if r == SITES:
        return 1
    return 2 * r if r > 0 else 1 - 2 * r


PLACES = ((0, 2, -2, 4), (1, -1, 3, -3))


def kernel(
    sections,
    seq_count,
    fresh,
    stale,
    gains_in,
    hidden,
    gate,
    patch,
    step,
    out,
    raw,
    old,
    gains,
    gate_cols,
    gate_row,
    q_out,
    kv_out,
    q_home,
    h_in,
    k_mine,
    v_mine,
    q_site,
    k_site,
    v_site,
    kv_new,
    part,
    send,
    mid,
    back,
    mixed,
    local_sem,
    first_send,
    first_recv,
    new_send,
    new_recv,
    kv_send,
    kv_recv,
    q_send,
    q_recv,
    back_send,
    back_recv,
    mid_send,
    mid_recv,
    out_send,
    out_recv,
):
    groups = HEAD_GROUPS
    ring = seq_count // groups
    heads = q_out.shape[1]
    toks = q_out.shape[2]
    dim = HEAD_DIM
    width = heads * dim
    block = groups * toks
    rows = old.shape[1]
    kept = old.shape[0] - 1
    tall = send.shape[2]
    stale_keys = kept * rows
    last = (kept - 1) * rows
    before_at, after_at, fresh_at = stale_keys, stale_keys + last, 2 * stale_keys

    sec = lax.axis_index("section")
    me = lax.axis_index("seq")
    y = me // groups
    a = me % groups
    next_sec = lax.rem(sec + 1, sections)
    prev_sec = lax.rem(sec + sections - 1, sections)
    core = lax.rem(a, 2)
    parity = lax.rem(y, 2)

    def duty_of(parity, core):
        count = 1 + jnp.where(parity == core, 1, 0)
        return parity * (heads - count), count

    first_head, duty_count = duty_of(parity, core)

    def away(i, core=core):
        return lax.rem((i + core) // 2 + parity, 2)

    def flipped(d):
        bits = [1 << n for n in range(groups.bit_length() - 1)]
        return sum(
            bit * (1 - lax.rem(a // bit, 2) if d & bit else lax.rem(a // bit, 2)) for bit in bits
        )

    def along(r, d=0):
        return lax.rem(y + ring + r, ring) * groups + flipped(d)

    def peer(d):
        return along(0, d)

    pair, side = a // 2, a // (groups // 2)
    pieces = [
        pl.ds(pl.multiple_of(start * toks, toks), count * toks)
        for start, count in (
            (2 * pair, 2),
            (2 * (pair + 1 - 2 * lax.rem(pair, 2)), 2),
            ((1 - side) * (groups // 2), groups // 2),
        )
    ]

    far_first = sorted(range(groups), key=lambda d: -(d // 2 == 2) * 2 - (d > 1))

    barrier = pltpu.get_barrier_semaphore()

    def greet(section, seq):
        pl.semaphore_signal(barrier, inc=1, device_id=(section, seq), device_id_type=MESH)

    for d in far_first:
        greet(sec, along(1, d))
        if d:
            greet(sec, along(0, d))
        if d == far_first[1]:
            greet(sec, along(4))
    for r in (3, -3, 2, -2, -1):
        greet(sec, along(r))
    greet(prev_sec, me)
    greeted = 2 * groups + 6

    mine = pl.ds(pl.multiple_of(a * toks, toks), toks)
    my_cols = pl.ds(pl.multiple_of(a * width, dim), width)
    loads = [
        pltpu.make_async_copy(src, dst, local_sem.at[n])
        for n, (src, dst) in enumerate(
            (
                (gains_in.at[0], gains),
                (fresh.at[0], raw),
                (stale.at[0, 0], old),
                (hidden.at[0, :, my_cols], h_in.at[mine]),
                (gate.at[0, :, my_cols], gate_cols),
            )
        )
    ]
    got_gains, got_raw, got_old, got_h, got_gate = loads
    for load in loads:
        load.start()

    def normed(which, g, i):
        col = (g * heads + i) * dim
        x = raw[which, :, col : col + dim].astype(F32)
        factor = lax.rsqrt(jnp.mean(x * x, axis=-1, keepdims=True) + 1e-06)
        return (x * factor * gains[which : which + 1, :]).astype(BF16)

    got_gains.wait()
    got_raw.wait()
    for g in range(groups):
        for i in range(heads):
            q_out[g, i] = normed(0, g, i)
    for g in range(groups):
        for i in range(heads):
            col = (g * heads + i) * dim
            kv_out[g, i, 0] = normed(1, g, i)
            kv_out[g, i, 1] = raw[2, :, col : col + dim]
    q_home[:, mine, :] = q_out[a]

    got_old.wait()
    skip = patch[0]
    for n in range(kept):
        m = n + (n >= skip).astype(jnp.int32)
        spot = slice(n * rows, (n + 1) * rows)
        for i in range(heads):
            k_mine[i, spot, :] = old[m, :, i * dim : (i + 1) * dim]
            v_mine[i, :, spot] = old[m, :, width + i * dim : width + (i + 1) * dim].T

    pl.semaphore_wait(barrier, greeted)

    def first_copy(kind, d):
        to = flipped(d)
        cols = pl.ds(pl.multiple_of(to * width, dim), width)
        src, dst = (
            (lambda: q_out.at[to], lambda: q_home.at[:, mine, :]),
            (lambda: hidden.at[0, :, cols], lambda: h_in.at[mine]),
        )[kind]
        return pltpu.make_async_remote_copy(
            src_ref=src(),
            dst_ref=dst(),
            send_sem=first_send.at[kind, d],
            recv_sem=first_recv.at[kind, d],
            device_id=(sec, peer(d)),
            device_id_type=MESH,
        )

    def arrived(dst, sem):
        pltpu.make_async_remote_copy(
            src_ref=dst,
            dst_ref=dst,
            send_sem=first_send.at[0, 0],
            recv_sem=sem,
            device_id=(sec, peer(1)),
            device_id_type=MESH,
        ).wait_recv()

    def first_arrived(kind, d):
        source = flipped(d)
        spot = pl.ds(pl.multiple_of(source * toks, toks), toks)
        dst = (lambda: q_home.at[:, spot, :], lambda: h_in.at[spot])[kind]()
        arrived(dst, first_recv.at[kind, d])

    def new_copy(d, off, count):
        to = flipped(d)
        first, _ = duty_of(lax.rem(parity + off, 2), lax.rem(to, 2))
        spot = pl.ds(pl.multiple_of(off * block + a * toks, toks), toks)
        return pltpu.make_async_remote_copy(
            src_ref=kv_out.at[to, pl.ds(first, count)],
            dst_ref=kv_new.at[pl.ds(0, count), :, spot, :],
            send_sem=new_send.at[d, off],
            recv_sem=new_recv.at[0],
            device_id=(sec, along(-off, d)),
            device_id_type=MESH,
        )

    def each_new(act):
        for d in range(groups):
            for off in range(2):
                if d or off:
                    for count in (1, 2):

                        @pl.when(duty_of(lax.rem(parity + off, 2), lax.rem(a + d, 2))[1] == count)
                        def _(d=d, off=off, count=count):
                            act(new_copy(d, off, count))

    for d in range(1, groups):
        first_copy(0, d).start()

    def stale_copies(i):
        there, _ = duty_of(1 - parity, core)
        j = i - there
        head, tail = pl.ds(0, last), pl.ds(last, rows)
        head_at, tail_at = pl.ds(before_at, last), pl.ds(after_at, rows)
        deep = pl.ds(0, dim)
        return [
            pltpu.make_async_remote_copy(
                src_ref=src,
                dst_ref=dst,
                send_sem=kv_send.at[i, n],
                recv_sem=kv_recv.at[j, n],
                device_id=(sec, along(places)),
                device_id_type=MESH,
            )
            for n, (src, dst, places) in enumerate(
                (
                    (k_mine.at[i, head, :], k_site.at[j, head_at, :], 1),
                    (v_mine.at[i, :, head], v_site.at[j, deep, head_at], 1),
                    (k_mine.at[i, tail, :], k_site.at[j, tail_at, :], -1),
                    (v_mine.at[i, :, tail], v_site.at[j, deep, tail_at], -1),
                )
            )
        ]

    for i in range(heads):

        @pl.when(away(i) == 1)
        def _(i=i):
            for copy in stale_copies(i):
                copy.start()
            back[i, 2] = jnp.zeros_like(back[i, 2])

    def own_part(j, carry):
        k_site[j, 0:stale_keys, :] = k_mine[first_head + j]
        v_site[j, 0:dim, 0:stale_keys] = v_mine[first_head + j]
        v_site[j, dim:, :] = jnp.ones_like(v_site[j, dim:, :])
        kv_new[j, :, mine, :] = kv_out[a, first_head + j]
        return carry

    lax.fori_loop(0, duty_count, own_part, 0)
    each_new(lambda copy: copy.start())

    def q_copy(i, off, k, piece):
        places = PLACES[off][k]
        there, _ = duty_of(lax.rem(parity + off, 2), core)
        j, slot = i - there, slot_of(SITES if places == SITES else -places)
        return pltpu.make_async_remote_copy(
            src_ref=q_home.at[i, pieces[piece], :],
            dst_ref=q_site.at[j, slot, pieces[piece], :],
            send_sem=q_send.at[i, k, piece],
            recv_sem=q_recv.at[j, slot, piece],
            device_id=(sec, along(places)),
            device_id_type=MESH,
        )

    def each_q(piece, act, order=(3, 2, 1, 0)):
        for k in order:
            for i in range(heads):
                for off in range(2):
                    if PLACES[off][k]:

                        @pl.when(away(i) == off)
                        def _(i=i, off=off, k=k):
                            act(q_copy(i, off, k, piece))

    for piece, low, high in ((0, 1, 2), (1, 2, 4), (2, 4, groups)):
        for d in range(low, high):
            first_arrived(0, d)
        each_q(piece, lambda copy: copy.start(), (3, 2) if piece else (3, 2, 1, 0))
    for piece in (1, 2):
        each_q(piece, lambda copy: copy.start(), (1, 0))
    for d in range(1, groups):
        first_copy(1, d).start()

    def own_block(j, carry):
        q_site[j, 0] = q_home[first_head + j]
        return carry

    lax.fori_loop(0, duty_count, own_block, 0)

    got_gate.wait()
    picked = lax.broadcasted_iota(jnp.int32, gate_cols.shape, 0) == step[0]
    gate_row[...] = jnp.sum(
        jnp.where(picked, gate_cols[...].astype(F32), 0.0), axis=0, keepdims=True
    )

    def attend(p, j):
        q = q_site[j, 2 * p : 2 * p + 2].reshape(2 * block, dim)
        scores = lax.dot_general(
            k_site[j], q, (((1,), (1,)), ((), ())), preferred_element_type=F32
        )
        weights = jnp.exp(scores * (dim ** (-0.5))).astype(BF16)
        return jnp.dot(v_site[j], weights, preferred_element_type=F32)

    near = (2, -2, 1, -1)
    cut = dim // 2

    def back_copy(j, r):
        k = PLACES[r % 2].index(-r)
        return pltpu.make_async_remote_copy(
            src_ref=send.at[j, slot_of(r)],
            dst_ref=back.at[first_head + j, k],
            send_sem=back_send.at[j, slot_of(r)],
            recv_sem=back_recv.at[first_head + j, k],
            device_id=(sec, along(r)),
            device_id_type=MESH,
        )

    hops = (
        (SITES, 2, 2, pl.ds(0, cut)),
        (SITES, -2, -2, pl.ds(cut, tall - cut)),
        (3, 2, 1, pl.ds(0, tall)),
        (-3, -2, -1, pl.ds(0, tall)),
    )

    def mid_copy(j, hop):
        r, way, there, spot = hops[hop]
        return pltpu.make_async_remote_copy(
            src_ref=send.at[j, slot_of(r), spot, :],
            dst_ref=mid.at[j, hop, spot, :],
            send_sem=mid_send.at[j, hop],
            recv_sem=mid_recv.at[j, hop],
            device_id=(sec, along(way)),
            device_id_type=MESH,
        )

    pairs = ((0, SITES), (1, -1), (2, -2), (3, -3))

    def keys_here(j, carry):
        head_at, tail_at = pl.ds(before_at, last), pl.ds(after_at, rows)
        arrived(k_site.at[j, head_at, :], kv_recv.at[j, 0])
        arrived(v_site.at[j, pl.ds(0, dim), head_at], kv_recv.at[j, 1])
        arrived(k_site.at[j, tail_at, :], kv_recv.at[j, 2])
        arrived(v_site.at[j, pl.ds(0, dim), tail_at], kv_recv.at[j, 3])
        return carry

    lax.fori_loop(0, duty_count, keys_here, 0)
    for count in (1, 2):

        @pl.when(duty_count == count)
        def _(count=count):
            arrived(kv_new.at[0:count, :, 0 : 2 * block - toks, :], new_recv.at[0])

    def fresh_here(j, carry):
        k_site[j, fresh_at:, :] = kv_new[j, 0]
        for n in range(2):
            spot = slice(n * block, (n + 1) * block)
            at = slice(fresh_at + n * block, fresh_at + (n + 1) * block)
            v_site[j, 0:dim, at] = kv_new[j, 1, spot, :].T
        return carry

    lax.fori_loop(0, duty_count, fresh_here, 0)

    for p in (0, 3, 2, 1):

        def work(j, carry, p=p):
            for r in pairs[p]:
                if r:
                    slot = slot_of(r)
                    for piece, spot in enumerate(pieces):
                        arrived(q_site.at[j, slot, spot, :], q_recv.at[j, slot, piece])
            total = attend(p, j)
            for n, r in enumerate(pairs[p]):
                sums = total[:, n * block : (n + 1) * block]
                if r == 0:
                    back[first_head + j, 0] = sums.astype(BF16)
                elif r in near:
                    part[j, near.index(r)] = sums
                else:
                    send[j, slot_of(r)] = sums.astype(BF16)
                    for hop in range(len(hops)):
                        if hops[hop][0] == r:
                            mid_copy(j, hop).start()
            return carry

        lax.fori_loop(0, duty_count, work, 0)

    for hop, (_, _, r, spot) in enumerate(hops):

        def add_on(j, carry, hop=hop, r=r, spot=spot):
            arrived(mid.at[j, hop, spot, :], mid_recv.at[j, hop])
            n = near.index(r)
            sums = part[j, n, spot, :] + mid[j, hop, spot, :].astype(F32)
            send[j, slot_of(r), spot, :] = sums.astype(BF16)
            if r == 2:
                send[j, slot_of(r), cut:, :] = part[j, n, cut:, :].astype(BF16)
            if r == -2:
                send[j, slot_of(r), 0:cut, :] = part[j, n, 0:cut, :].astype(BF16)
            back_copy(j, r).start()
            return carry

        lax.fori_loop(0, duty_count, add_on, 0)

    got_h.wait()
    for d in range(1, groups):
        first_arrived(1, d)

    def out_copy(i, d):
        to = flipped(d)
        spot = pl.ds(pl.multiple_of(to * toks, toks), toks)
        cols = pl.ds(pl.multiple_of(a * width + i * dim, dim), dim)
        return pltpu.make_async_remote_copy(
            src_ref=mixed.at[i, spot, :],
            dst_ref=out.at[0, :, cols],
            send_sem=out_send.at[i, d],
            recv_sem=out_recv.at[0],
            device_id=(next_sec, peer(d)),
            device_id_type=MESH,
        )

    for i in range(heads):
        pl.when(away(i) == 1)(lambda i=i: arrived(back.at[i, 0], back_recv.at[i, 0]))
        arrived(back.at[i, 1], back_recv.at[i, 1])
        pl.when(away(i) == 0)(lambda i=i: arrived(back.at[i, 2], back_recv.at[i, 2]))
        total = sum(back[i, k].astype(F32) for k in range(3))
        attention = (total[0:dim] / total[dim : dim + 1]).T
        attention = attention.astype(BF16).astype(F32)
        cols = slice(i * dim, (i + 1) * dim)
        mixed[i] = (h_in[:, cols].astype(F32) + gate_row[:, cols] * attention).astype(BF16)
        for d in far_first:
            out_copy(i, d).start()

    for kind in range(2):
        for d in range(1, groups):
            first_copy(kind, d).wait_send()
    each_new(lambda copy: copy.wait_send())
    for i in range(heads):

        @pl.when(away(i) == 1)
        def _(i=i):
            for copy in stale_copies(i):
                copy.wait_send()

    for piece in range(3):
        each_q(piece, lambda copy: copy.wait_send())

    def backs_sent(j, carry):
        for n in range(4):
            back_copy(j, near[n]).wait_send()
            mid_copy(j, n).wait_send()
        return carry

    lax.fori_loop(0, duty_count, backs_sent, 0)
    for i in range(heads):
        for d in range(groups):
            out_copy(i, d).wait_send()
    arrived(out, out_recv.at[0])


def shards(sections, fresh_qkv, stale_cache, norm_gains, hidden, gate_table, patch_index, step_index):
    seq_count = lax.axis_size("seq")
    groups = HEAD_GROUPS
    ring = seq_count // groups
    toks, full = hidden.shape[1:]
    width = full // groups
    heads = width // HEAD_DIM
    dim = HEAD_DIM
    block = toks * groups
    patches, rows = stale_cache.shape[2:4]
    stale_keys = (patches - 1) * rows
    tall = dim + 16
    fresh = fresh_qkv.transpose(0, 2, 1, 3)
    hbm = pl.BlockSpec(memory_space=pltpu.HBM)
    smem = pl.BlockSpec(memory_space=pltpu.SMEM)
    dma = pltpu.SemaphoreType.DMA
    return pl.pallas_call(
        functools.partial(kernel, sections, seq_count),
        out_shape=jax.ShapeDtypeStruct(hidden.shape, BF16),
        in_specs=[hbm] * 5 + [smem] * 2,
        out_specs=pl.BlockSpec(memory_space=pl.ANY),
        scratch_shapes=[
            pltpu.VMEM((3, toks, full), BF16),
            pltpu.VMEM((patches, rows, 2 * width), BF16),
            pltpu.VMEM((2, dim), F32),
            pltpu.VMEM((gate_table.shape[1], width), BF16),
            pltpu.VMEM((1, width), F32),
            pltpu.VMEM((groups, heads, toks, dim), BF16),
            pltpu.VMEM((groups, heads, 2, toks, dim), BF16),
            pltpu.VMEM((heads, block, dim), BF16),
            pltpu.VMEM((block, width), BF16),
            pltpu.VMEM((heads, stale_keys, dim), BF16),
            pltpu.VMEM((heads, dim, stale_keys), BF16),
            pltpu.VMEM((2, ring, block, dim), BF16),
            pltpu.VMEM((2, 2 * (stale_keys + block), dim), BF16),
            pltpu.VMEM((2, tall, 2 * (stale_keys + block)), BF16),
            pltpu.VMEM((2, 2, 2 * block, dim), BF16),
            pltpu.VMEM((2, 4, tall, block), F32),
            pltpu.VMEM((2, ring, tall, block), BF16),
            pltpu.VMEM((2, 4, tall, block), BF16),
            pltpu.VMEM((heads, 3, tall, block), BF16),
            pltpu.VMEM((heads, block, dim), BF16),
            dma((5,)),
            dma((2, groups)),
            dma((2, groups)),
            dma((groups, 2)),
            dma((1,)),
            dma((heads, 4)),
            dma((2, 4)),
            dma((heads, SITES, 3)),
            dma((2, ring, 3)),
            dma((2, ring)),
            dma((heads, 3)),
            dma((2, 4)),
            dma((2, 4)),
            dma((heads, groups)),
            dma((1,)),
        ],
        compiler_params=pltpu.CompilerParams(
            collective_id=0, has_side_effects=True, vmem_limit_bytes=24 * 1024 * 1024
        ),
    )(
        *(
            pltpu.with_memory_space_constraint(array, pltpu.HBM)
            for array in (
                fresh,
                stale_cache,
                norm_gains,
                hidden,
                gate_table,
            )
        ),
        patch_index,
        step_index,
    )


def solution(mesh):
    return jax.shard_map(
        functools.partial(shards, mesh.shape["section"]),
        mesh=mesh,
        in_specs=(
            P("section", "seq", None, None),
            P("section", "seq", None, None, None),
            P("section", None, None),
            P("section", "seq", None),
            P("section", None, None),
            P("section"),
            P("section"),
        ),
        out_specs=P("section", "seq", None),
        check_vma=False,
    )
```
